32 devices in a mesh: groups: 2 (over y), filt: 4 (over z), patch: 4 (over x, core).
Axes of the slice: x: 2, y: 2, z: 4, core: 2. Of those that a mesh axis runs over, the one named last changes fastest.
Arguments:
- activations: bfloat16 [8, 256, 4, 128, 128], P(('groups', 'patch'), None, None, 'filt'), parts along dimension 0, may hold values from -6 to 6
- filters: bfloat16 [3, 3, 3, 256, 256], replicated, may hold values from -0.078125 to 0.078125
- bias: bfloat16 [256], replicated, may hold values from -3 to 3
- cotangent: bfloat16 [8, 256, 4, 128, 128], P(('groups', 'patch'), None, None, 'filt'), parts along dimension 0, may hold values from -6 to 6
Outputs:
- output: bfloat16 [8, 256, 4, 128, 128], P(('groups', 'patch'), None, None, 'filt'), parts along dimension 0
- filter_grad: float32 [6, 3, 3, 256, 256], P('groups', None, None, None, 'filt'), parts along dimension 0
- bias_grad: float32 [512], P(('groups', 'filt')), parts along dimension 0
The draws below stay inside these ranges and needn't reach their ends.
There are 2 independent parts, one for each index of `groups`. The reference program is written for one: setup_inputs(seed, part) draws one part's arguments, and reference() takes and returns one part's arrays. A program takes and returns all parts, laid end to end along the dimension named above; an argument that names none is the same for every part. Nothing has to cross between parts.
All inputs are finite; a program needn't handle non-finite values.
Results may differ from the reference program's by a relative error of at most 0.001.
Values may be sent and summed in bfloat16 or wider, within the bound.
A program may use at most 640 MiB of HBM per device.

```python
import math
import jax
import jax.numpy as jnp
from jax import lax

CH = 256
DEP = 4
HH = 128
WW = 128
PATCHES = 4


def block_levels(own_key, dims, shards, smallest, high):
    def one(axis_at, blocks):
        heights = jax.random.uniform(jax.random.fold_in(jax.random.fold_in(own_key, 6), axis_at), (blocks,), jnp.float32, smallest / len(shards), high / len(shards))
        return jnp.repeat(jnp.exp(heights), dims[axis_at] // blocks).reshape((-1,) + (1,) * (len(dims) - axis_at - 1))

    loudness = one(*shards[0])
    for cut in shards[1:]:
        loudness = loudness * one(*cut)
    return loudness


def bell_draw(own_key, dims, width, reach, split=(), held_as=jnp.bfloat16):
    values = width * jax.random.normal(own_key, dims, jnp.float32)
    if split:
        values = values * block_levels(own_key, dims, split, -0.22, 0.18)
    return jnp.clip(values, -reach, reach).astype(held_as)


def setup_inputs(seed: int = 0, part: int = 0) -> dict:
    key_list = jax.random.split(jax.random.key(seed), 5)
    part_splits = jax.random.split(jax.random.fold_in(key_list[4], part), 5)
    return {
        "activations": bell_draw(part_splits[0], (PATCHES, CH, DEP, HH, WW), 1.0, 6.0, ((0, 4), (3, 4))),
        "filters": bell_draw(key_list[1], (3, 3, 3, CH, CH), (27 * CH) ** -0.5, 0.078125),
        "bias": bell_draw(key_list[2], (CH,), 0.5, 3.0),
        "cotangent": bell_draw(part_splits[3], (PATCHES, CH, DEP, HH, WW), 1.0, 6.0, ((0, 4), (3, 4))),
    }


def reference(activations, filters, bias, cotangent):
    inputs = activations.astype(jnp.float32)
    grads_in = cotangent.astype(jnp.float32)
    weights = filters.astype(jnp.float32)
    padded = jnp.pad(inputs, ((0, 0), (0, 0), (1, 1), (1, 1), (1, 1)))
    accum = jnp.zeros(grads_in.shape, jnp.float32)
    pieces = []
    for tap_a in range(3):
        for tap_b in range(3):
            for tap_c in range(3):
                window = padded[:, :, tap_a:tap_a + DEP, tap_b:tap_b + HH, tap_c:tap_c + WW]
                accum = accum + jnp.einsum('pidhw,io->podhw', window, weights[tap_a, tap_b, tap_c])
                pieces.append(jnp.einsum('pidhw,podhw->io', window, grads_in))
    output = (accum + bias.astype(jnp.float32)[None, :, None, None, None]).astype(jnp.bfloat16)
    scale = jnp.float32(1.0 / math.sqrt(PATCHES * DEP * HH * WW))
    filter_grad = jnp.stack(pieces).reshape(3, 3, 3, CH, CH) * scale
    bias_grad = lax.optimization_barrier(jnp.sum(grads_in, axis=(0, 2, 3, 4))) * scale
    return (output, filter_grad, bias_grad)
```

```python
import functools
import math

import jax
import jax.numpy as jnp
from jax import lax
from jax.experimental import pallas as pl
from jax.experimental.pallas import tpu as pltpu
from jax.sharding import PartitionSpec as P

LANES = 128
PARAMS = pltpu.CompilerParams(vmem_limit_bytes=60 << 20)


def shifted(cells, tap):
    if tap == 1:
        return cells
    rows, lanes = cells.shape
    lane = lax.broadcasted_iota(jnp.int32, (rows, LANES), 1)
    groups = []
    for at in range(0, lanes, LANES):
        group = pltpu.roll(cells[:, at : at + LANES], 1 if tap == 0 else LANES - 1, 1)
        groups.append(
            jnp.where(lane == (0 if tap == 0 else LANES - 1), jnp.zeros_like(group), group)
        )
    return jnp.concatenate(groups, axis=1)


def flat_kernel(x_ref, o_ref):
    for row in range(x_ref.shape[3]):
        o_ref[0, :, row * LANES : (row + 1) * LANES] = x_ref[0, :, 0, row, :]


def flat(cells):
    _, channels, depth, rows, width = cells.shape
    return pl.pallas_call(
        flat_kernel,
        grid=(depth,),
        in_specs=[pl.BlockSpec((1, channels, 1, rows, width), lambda d: (0, 0, d, 0, 0))],
        out_specs=pl.BlockSpec((1, channels, rows * width), lambda d: (d, 0, 0)),
        out_shape=jax.ShapeDtypeStruct((depth, channels, rows * width), cells.dtype),
        compiler_params=PARAMS,
        cost_estimate=pl.CostEstimate(
            flops=0, bytes_accessed=12 * cells.size, transcendentals=0
        ),
        name="flat",
    )(cells)


def flat_rimmed_kernel(x_ref, above_ref, below_ref, o_ref):
    rows = x_ref.shape[3]
    o_ref[0, :, :LANES] = above_ref[0, :, 0, 0, :]
    for row in range(rows):
        o_ref[0, :, (row + 1) * LANES : (row + 2) * LANES] = x_ref[0, :, 0, row, :]
    o_ref[0, :, (rows + 1) * LANES :] = below_ref[0, :, 0, 0, :]


def flat_rimmed(cells, above, below):
    _, channels, depth, rows, width = cells.shape
    edge = pl.BlockSpec((1, channels, 1, 1, width), lambda d: (0, 0, d, 0, 0))
    return pl.pallas_call(
        flat_rimmed_kernel,
        grid=(depth,),
        in_specs=[
            pl.BlockSpec((1, channels, 1, rows, width), lambda d: (0, 0, d, 0, 0)),
            edge,
            edge,
        ],
        out_specs=pl.BlockSpec((1, channels, (rows + 2) * width), lambda d: (d, 0, 0)),
        out_shape=jax.ShapeDtypeStruct((depth, channels, (rows + 2) * width), cells.dtype),
        compiler_params=PARAMS,
        cost_estimate=pl.CostEstimate(
            flops=0, bytes_accessed=12 * cells.size, transcendentals=0
        ),
        name="flat_rimmed",
    )(cells, above, below)


def slabs(depth, channels, lanes):
    return [
        pl.BlockSpec(
            (1, channels, lanes), lambda d, o=o: (jnp.clip(d + o, 0, depth - 1), 0, 0)
        )
        for o in (-1, 0, 1)
    ]


def grad_kernel(tap_c, depth, before, here, after, cot_ref, out_ref, moved, total, bias_sum):
    d = pl.program_id(0)
    channels, lanes = cot_ref.shape[1:]
    moved[...] = shifted(cot_ref[0], 2 - tap_c)

    @pl.when(d == 0)
    def _():
        total[...] = jnp.zeros_like(total)
        bias_sum[...] = jnp.zeros_like(bias_sum)

    if tap_c == 1:
        part = bias_sum[...]
        for at in range(0, lanes, LANES):
            part = part + cot_ref[0, :, at : at + LANES].astype(jnp.float32)
        bias_sum[...] = part

    def taps(tap_a, slab):
        for tap_b in range(3):
            total[tap_a * 3 + tap_b] += lax.dot_general(
                slab[0, :, tap_b * LANES : tap_b * LANES + lanes],
                moved[...],
                (((1,), (1,)), ((), ())),
                preferred_element_type=jnp.float32,
            )

    pl.when(d > 0)(lambda: taps(0, before))
    taps(1, here)
    pl.when(d < depth - 1)(lambda: taps(2, after))

    @pl.when(d == depth - 1)
    def _():
        for tap in range(9):
            out_ref[:, tap * channels : (tap + 1) * channels] = total[tap].T
        if tap_c == 1:
            out_ref[:, 9 * channels :] = bias_sum[...]


def grad(tap_c, cells, cot):
    depth, channels, lanes = cot.shape
    wide = 9 * channels + (LANES if tap_c == 1 else 0)
    return pl.pallas_call(
        functools.partial(grad_kernel, tap_c, depth),
        grid=(depth,),
        in_specs=slabs(depth, channels, cells.shape[2])
        + [pl.BlockSpec((1, channels, lanes), lambda d: (d, 0, 0))],
        out_specs=pl.BlockSpec((channels, wide), lambda d: (0, 0)),
        out_shape=jax.ShapeDtypeStruct((channels, wide), jnp.float32),
        scratch_shapes=[
            pltpu.VMEM((channels, lanes), cot.dtype),
            pltpu.VMEM((9, channels, channels), jnp.float32),
            pltpu.VMEM((channels, LANES), jnp.float32),
        ],
        compiler_params=PARAMS,
        cost_estimate=pl.CostEstimate(
            flops=18 * channels * channels * depth * lanes,
            bytes_accessed=8 * cells.size,
            transcendentals=0,
        ),
        name=f"grad_{tap_c}",
    )(cells, cells, cells, cot)


def forward_kernel(depth, tile, before, here, after, weight_ref, bias_ref, out_ref):
    d = pl.program_id(0)
    channels, rows = out_ref.shape[1], out_ref.shape[3]
    deep = 3 * channels

    def run(refs, first, last):
        weights = weight_ref[:, first:last]

        def body(t, _):
            base = pl.multiple_of(t * tile, tile)
            window = jnp.concatenate(
                [r[0, :, pl.ds(base + b * LANES, tile)] for r in refs for b in range(3)], axis=0
            )
            parts = lax.dot_general(
                weights,
                window,
                (((1,), (0,)), ((), ())),
                preferred_element_type=jnp.float32,
            )
            sums = (
                parts[channels : 2 * channels]
                + shifted(parts[:channels], 0)
                + shifted(parts[2 * channels :], 2)
                + bias_ref[...]
            )
            high = tile // LANES
            at = pl.multiple_of(t * high, high)
            out_ref[0, :, 0, pl.ds(at, high), :] = sums.astype(out_ref.dtype).reshape(
                channels, high, LANES
            )
            return 0

        lax.fori_loop(0, rows * LANES // tile, body, 0)

    pl.when(d == 0)(lambda: run((here, after), deep, 3 * deep))
    pl.when((d > 0) & (d < depth - 1))(lambda: run((before, here, after), 0, 3 * deep))
    pl.when(d == depth - 1)(lambda: run((before, here), 0, 2 * deep))


def forward(cells, weights, bias, rows):
    depth, channels, rimmed = cells.shape
    tile = LANES * min(rows, 16)
    return pl.pallas_call(
        functools.partial(forward_kernel, depth, tile),
        grid=(depth,),
        in_specs=slabs(depth, channels, rimmed)
        + [
            pl.BlockSpec(weights.shape, lambda d: (0, 0)),
            pl.BlockSpec(bias.shape, lambda d: (0, 0)),
        ],
        out_specs=pl.BlockSpec((1, channels, 1, rows, LANES), lambda d: (0, 0, d, 0, 0)),
        out_shape=jax.ShapeDtypeStruct((1, channels, depth, rows, LANES), jnp.bfloat16),
        compiler_params=PARAMS,
        cost_estimate=pl.CostEstimate(
            flops=54 * channels * channels * depth * rows * LANES,
            bytes_accessed=10 * cells.size,
            transcendentals=0,
        ),
        name="forward",
    )(cells, cells, cells, weights, bias)


def finish_kernel(scale, first, middle, last, grad_ref, bias_ref):
    channels = grad_ref.shape[3]
    for tap_c, ref in enumerate((first, middle, last)):
        for tap in range(9):
            grad_ref[tap // 3, tap % 3, tap_c] = (
                ref[:, tap * channels : (tap + 1) * channels].T * scale
            )
    bias_ref[...] = jnp.sum(middle[:, 9 * channels :], axis=1, keepdims=True) * scale


def finish(scale, pieces, channels):
    owned = pieces[0].shape[0]
    return pl.pallas_call(
        functools.partial(finish_kernel, scale),
        out_shape=(
            jax.ShapeDtypeStruct((3, 3, 3, channels, owned), jnp.float32),
            jax.ShapeDtypeStruct((owned, 1), jnp.float32),
        ),
        compiler_params=PARAMS,
        name="finish",
    )(*pieces)


def local(activations, filters, bias, cotangent):
    count, channels, depth, rows, width = activations.shape
    bands = lax.axis_size("filt")
    scale = 1.0 / math.sqrt(count * lax.axis_size("patch") * depth * rows * bands * width)
    above = lax.ppermute(
        activations[:, :, :, rows - 1 :], "filt", [(i, i + 1) for i in range(bands - 1)]
    )
    below = lax.ppermute(
        activations[:, :, :, :1], "filt", [(i + 1, i) for i in range(bands - 1)]
    )
    cot = flat(cotangent)
    cells = flat_rimmed(activations, above, below)
    pieces = []
    for tap_c in range(3):
        terms = grad(tap_c, cells, cot)
        terms = lax.psum_scatter(terms, ("filt", "patch"), scatter_dimension=0, tiled=True)
        pieces.append(lax.all_gather(terms, "patch", axis=0, tiled=True))
    weights = jnp.transpose(filters, (2, 4, 0, 1, 3)).reshape(3 * channels, 9 * channels)
    output = forward(cells, weights, bias.astype(jnp.float32)[:, None], rows)
    filter_grad, bias_grad = finish(scale, pieces, channels)
    return (output, filter_grad, bias_grad[:, 0])


def solution(mesh):
    return jax.shard_map(
        local,
        mesh=mesh,
        in_specs=(
            P(("groups", "patch"), None, None, "filt", None),
            P(),
            P(),
            P(("groups", "patch"), None, None, "filt", None),
        ),
        out_specs=(
            P(("groups", "patch"), None, None, "filt", None),
            P("groups", None, None, None, "filt"),
            P(("groups", "filt")),
        ),
        check_vma=False,
    )
```
